32 devices in a mesh: groups: 2 (over x), dp: 8 (over z, y), mat: 2 (over core).
Axes of the slice: x: 2, y: 2, z: 4, core: 2. Of those that a mesh axis runs over, the one named last changes fastest.
Arguments:
- in_factor: bfloat16 [256, 8, 64, 128], P(('groups', 'dp'), None, 'mat'), parts along dimension 0, may hold values from -6 to 6
- out_factor: bfloat16 [256, 8, 64, 128], P(('groups', 'dp')), parts along dimension 0, may hold values from -6 to 6
- seq_lengths: int32 [256], P(('groups', 'dp')), parts along dimension 0, may hold values from 1 to 128, 10240 in all
- sequence_ids: int32 [256], P('groups'), parts along dimension 0, may hold values from 0 to 127, each once
- matrix_owner: int32 [8], replicated, may hold values from 0 to 7, each once
- queries: bfloat16 [8, 512, 4096], P('dp', None, 'mat'), may hold values from -0.03125 to 0.03125
Outputs:
- fisher: bfloat16 [16, 4096, 4096], P(('groups', 'dp'), 'mat'), parts along dimension 0
- scores: float32 [256, 512], P(('groups', 'dp', 'mat')), parts along dimension 0
The draws below stay inside these ranges and needn't reach their ends.
There are 2 independent parts, one for each index of `groups`. The reference program is written for one: setup_inputs(seed, part) draws one part's arguments, and reference() takes and returns one part's arrays. A program takes and returns all parts, laid end to end along the dimension named above; an argument that names none is the same for every part. Nothing has to cross between parts.
Inputs may be any that keep to these rules, and one draw needn't show every extreme that they name: `sequence_ids`: each value once. `matrix_owner`: each value once.
All inputs are finite; a program needn't handle non-finite values. No bound on the sum of `seq_lengths` on one device may be relied on, other than what follows from the above.
Results may differ from the reference program's by a relative error of at most 0.0057.
Values may be sent and summed in bfloat16 or wider, within the bound.
No kernel may reach another device: no remote copies, remote signals or barrier semaphores. Data moves between devices by JAX's collectives and lax.ppermute only.
A program may use at most 128 MiB of HBM per device.

```python
import math
import jax
import jax.numpy as jnp
import numpy as np
from jax import lax

PROJ = 64
VEC = 4096
SEQS = 128
LEN = 128
QUERIES = 512
MATRICES = 8


def block_scale(key, dims, pieces, low, largest):
    level, own = 1.0, jax.random.fold_in(key, 6)
    for axis_at, parts in pieces:
        steps = jnp.exp(jax.random.uniform(jax.random.fold_in(own, axis_at), (parts,), jnp.float32, low / len(pieces), largest / len(pieces)))
        level = level * jnp.repeat(steps, dims[axis_at] // parts).reshape([-1 if axis == axis_at else 1 for axis in range(len(dims))])
    return level


def split_up(amount, total, reach, lean):
    portions = [(1 << 20) // math.isqrt(grade ** lean) + 1 for grade in range(2, amount + 1)]
    spare, given = total - reach - (amount - 1), [1] * (amount - 1)
    while spare > 0:
        candidates = [i for i in range(amount - 1) if given[i] < reach]
        pool, budget = sum([portions[i] for i in candidates]), spare
        for i in candidates:
            addition = min(reach - given[i], max(1, budget * portions[i] // pool), spare)
            given[i] = given[i] + addition
            spare = spare - addition
    return np.array([reach] + given)


def ragged(stream_key, count, total, most, skew):
    if count == 2:
        one = jax.random.randint(stream_key, (), max(1, total - most), min(most, total - 1) + 1)
        return jnp.stack([one, total - one])
    lengths = jnp.asarray(split_up(count, total, most, skew), jnp.int32)
    couples = (count - 1) // 2
    giver, taker = lengths[1:1 + 2 * couples:2], lengths[2:2 + 2 * couples:2]
    room = jnp.minimum(giver - 1, most - taker)
    shifted = jax.random.randint(jax.random.fold_in(stream_key, 1), (couples,), 0, 1 << 20) % (room + 1)
    lengths = lengths.at[1:1 + 2 * couples:2].set(giver - shifted).at[2:2 + 2 * couples:2].set(taker + shifted)
    return lengths[jax.random.permutation(jax.random.fold_in(stream_key, 2), count)]


def normal_values(stream_key, shape, scale, reach, shards=(), kind=jnp.bfloat16):
    values = jax.random.normal(stream_key, shape, jnp.float32) * scale
    if len(shards) > 0:
        values = block_scale(stream_key, shape, shards, -0.22, 0.18) * values
    return jnp.clip(values, min=-reach, max=reach).astype(kind)


def setup_inputs(seed: int = 0, part: int = 0) -> dict:
    keys = jax.random.split(jax.random.key(seed), 7)
    part_keys = jax.random.split(jax.random.fold_in(keys[6], part), 7)
    return {
        "in_factor": normal_values(part_keys[0], (SEQS, MATRICES, PROJ, LEN), 1.0, 6.0, ((0, 8), (2, 2))),
        "out_factor": normal_values(part_keys[1], (SEQS, MATRICES, PROJ, LEN), 1.0, 6.0, ((0, 8),)),
        "seq_lengths": ragged(part_keys[2], SEQS, SEQS * LEN * 5 // 8, LEN, 2).astype(jnp.int32),
        "sequence_ids": jax.random.permutation(part_keys[3], SEQS).astype(jnp.int32),
        "matrix_owner": jax.random.permutation(keys[4], MATRICES).astype(jnp.int32),
        "queries": normal_values(keys[5], (MATRICES, QUERIES, VEC), (MATRICES * VEC) ** -0.5, 0.03125, ((0, 8), (2, 2))),
    }


def reference(in_factor, out_factor, seq_lengths, sequence_ids, matrix_owner, queries):
    positions = jnp.arange(LEN, dtype=jnp.int32)
    token_mask = (positions[None, :] < seq_lengths[:, None]).astype(jnp.float32)
    weighted = out_factor.astype(jnp.float32) * token_mask[:, None, None, :]
    grad_tiles = jnp.einsum("smit,smot->smio", in_factor.astype(jnp.float32), weighted, precision=lax.Precision.HIGHEST) * (LEN ** -0.5)
    gradients = grad_tiles.reshape(SEQS, MATRICES, VEC).astype(jnp.bfloat16)
    slot_matrix = jnp.zeros((MATRICES,), jnp.int32).at[matrix_owner].set(jnp.arange(MATRICES, dtype=jnp.int32))
    slot_grads = jnp.take(gradients, slot_matrix, axis=1)

    def fisher_one(slot_block):
        return (jnp.dot(slot_block.T, slot_block, preferred_element_type=jnp.float32) / SEQS).astype(jnp.bfloat16)

    fisher = lax.map(fisher_one, jnp.moveaxis(slot_grads, 1, 0))
    arrival = jnp.einsum("rkj,kqj->rq", slot_grads.astype(jnp.float32), queries.astype(jnp.float32), precision=lax.Precision.HIGHEST)
    inverse = jnp.zeros((SEQS,), jnp.int32).at[sequence_ids].set(jnp.arange(SEQS, dtype=jnp.int32))
    scores = jnp.take(arrival, inverse, axis=0)
    return fisher, scores
```

```python
import functools

import jax
import jax.numpy as jnp
from jax import lax
from jax.experimental import pallas as pl
from jax.experimental.pallas import tpu as pltpu
from jax.sharding import PartitionSpec as P

NT = (((1,), (1,)), ((), ()))
TN = (((0,), (0,)), ((), ()))


def grad_body(owner, lengths, in_ref, out_ref, grad_ref, tiles):
    seqs, _, rows, length = in_ref.shape
    width = out_ref.shape[2]
    per = length // width
    scale = length ** (-0.5)
    lane = lax.broadcasted_iota(jnp.int32, (1, length), 1)
    for s in range(seqs):
        left = jnp.where(lane < lengths[s], in_ref[s, 0], 0)
        right = out_ref[s, 0]
        right = jnp.concatenate([right] * per, axis=0)
        tiles[s * rows:(s + 1) * rows, :] = lax.dot_general(
            left, right, NT, preferred_element_type=jnp.float32
        )
    for t in range(rows // per):
        tile = tiles[pl.ds(per * t, seqs, stride=rows), :]
        for p in range(1, per):
            other = tiles[pl.ds(per * t + p, seqs, stride=rows), :]
            tile = jnp.where(lane < p * width, tile, other)
        grad_ref[0, :, t * length:(t + 1) * length] = (tile * scale).astype(grad_ref.dtype)


def gradients(in_factor, out_factor, seq_lengths, matrix_owner):
    seqs, matrices, rows, length = in_factor.shape
    width = out_factor.shape[2]
    return pl.pallas_call(
        grad_body,
        out_shape=jax.ShapeDtypeStruct((matrices, seqs, rows * width), jnp.bfloat16),
        grid_spec=pltpu.PrefetchScalarGridSpec(
            num_scalar_prefetch=2,
            grid=(matrices,),
            in_specs=[
                pl.BlockSpec((seqs, 1, rows, length), lambda m, owner, lens: (0, m, 0, 0)),
                pl.BlockSpec((seqs, 1, width, length), lambda m, owner, lens: (0, m, 0, 0)),
            ],
            out_specs=pl.BlockSpec((1, seqs, rows * width), lambda m, owner, lens: (owner[m], 0, 0)),
            scratch_shapes=[pltpu.VMEM((seqs * rows, length), jnp.float32)],
        ),
        compiler_params=pltpu.CompilerParams(vmem_limit_bytes=32 << 20),
        name="gradients",
    )(matrix_owner, seq_lengths, in_factor, out_factor)


def score_body(rows_each, first, cores, core, ids, x_ref, q_ref, *refs):
    s_ref = refs[-1]
    rows = s_ref.shape[0]
    total = ids.shape[1]

    @pl.when(pl.program_id(0) == 0)
    def _():
        s_ref[...] = jnp.zeros_like(s_ref) if first else refs[0][...]

    at = lax.broadcasted_iota(jnp.int32, (rows, total), 0)
    wanted = (at // rows_each * cores + core[0]) * rows_each + at % rows_each
    pick = jnp.where(wanted == ids[...], 1.0, 0.0).astype(jnp.bfloat16)
    picked = jnp.dot(pick, x_ref[...], preferred_element_type=jnp.float32).astype(jnp.bfloat16)
    s_ref[...] += lax.dot_general(picked, q_ref[...], NT, preferred_element_type=jnp.float32)


def partial_scores(core, ids, x, q, before, rows, rows_each, cores):
    total, half = x.shape
    queries = q.shape[0]
    step = 512 if half % 512 == 0 else half
    whole = pl.BlockSpec((rows, queries), lambda k, core: (0, 0))
    extra = () if before is None else (before,)
    return pl.pallas_call(
        functools.partial(score_body, rows_each, before is None, cores),
        out_shape=jax.ShapeDtypeStruct((rows, queries), jnp.float32),
        grid_spec=pltpu.PrefetchScalarGridSpec(
            num_scalar_prefetch=1,
            grid=(half // step,),
            in_specs=[
                pl.BlockSpec((1, total), lambda k, core: (0, 0)),
                pl.BlockSpec((total, step), lambda k, core: (0, k)),
                pl.BlockSpec((queries, step), lambda k, core: (0, k)),
            ]
            + [whole] * len(extra),
            out_specs=whole,
        ),
        compiler_params=pltpu.CompilerParams(vmem_limit_bytes=32 << 20),
        cost_estimate=pl.CostEstimate(
            flops=2 * rows * queries * half, bytes_accessed=2 * half * (queries + total), transcendentals=0
        ),
        name="scores",
    )(core, ids, x, q, *extra)


def fisher_body(total, core, left_ref, own_ref, other_ref, f_ref):
    half = own_ref.shape[1]
    step = 1024 if half % 1024 == 0 else half
    for place, ref in ((core[0], own_ref), (1 - core[0], other_ref)):
        for at in range(0, half, step):
            block = lax.dot_general(
                left_ref[...], ref[:, at:at + step], TN, preferred_element_type=jnp.float32
            )
            where = pl.ds(pl.multiple_of(place * half + at, 128), step)
            f_ref[0, :, where] = (block * (1.0 / total)).astype(f_ref.dtype)


def fisher_block(core, own, other):
    total, half = own.shape
    step = 256 if half % 256 == 0 else half
    return pl.pallas_call(
        functools.partial(fisher_body, total),
        out_shape=jax.ShapeDtypeStruct((1, half, 2 * half), jnp.bfloat16),
        grid_spec=pltpu.PrefetchScalarGridSpec(
            num_scalar_prefetch=1,
            grid=(half // step,),
            in_specs=[
                pl.BlockSpec((total, step), lambda r, core: (0, r)),
                pl.BlockSpec((total, half), lambda r, core: (0, 0)),
                pl.BlockSpec((total, half), lambda r, core: (0, 0)),
            ],
            out_specs=pl.BlockSpec((1, step, 2 * half), lambda r, core: (0, r, 0)),
        ),
        compiler_params=pltpu.CompilerParams(vmem_limit_bytes=48 << 20),
        cost_estimate=pl.CostEstimate(
            flops=4 * total * half * half, bytes_accessed=4 * half * (half + total), transcendentals=0
        ),
        name="fisher",
    )(core, own, own, other)


def local(dp, cores, in_factor, out_factor, seq_lengths, sequence_ids, matrix_owner, queries):
    swap = [(c, (c + 1) % cores) for c in range(cores)]
    core = lax.axis_index("mat").astype(jnp.int32)[None]
    own_q = queries[0]
    other_q = lax.ppermute(own_q, "mat", swap)
    grads = gradients(in_factor, out_factor, seq_lengths, matrix_owner)
    seqs, half = grads.shape[1:]
    own = lax.all_to_all(grads, "dp", split_axis=0, concat_axis=0, tiled=True)
    total = dp * seqs
    own = own.reshape(total, half)
    other = lax.ppermute(own, "mat", swap)
    rows = total // cores
    rows_each = rows // dp
    ids = sequence_ids[None, :]
    part = partial_scores(core, ids, own, own_q, None, rows, rows_each, cores)
    part = partial_scores(core, ids, other, other_q, part, rows, rows_each, cores)
    parts = lax.all_to_all(part.reshape(dp, rows_each, -1), "dp", split_axis=0, concat_axis=0, tiled=True)
    fisher = fisher_block(core, own, other)
    return (fisher, jnp.sum(parts, axis=0))


def solution(mesh):
    in_specs = (
        P(("groups", "dp"), None, "mat", None),
        P(("groups", "dp"), None, None, None),
        P(("groups", "dp")),
        P("groups"),
        P(),
        P("dp", None, "mat"),
    )
    out_specs = (P(("groups", "dp"), "mat", None), P(("groups", "dp", "mat"), None))
    body = functools.partial(local, mesh.shape["dp"], mesh.shape["mat"])
    return jax.shard_map(body, mesh=mesh, in_specs=in_specs, out_specs=out_specs, check_vma=False)
```

```python
import functools

import jax
import jax.numpy as jnp
from jax import lax
from jax.experimental import pallas as pl
from jax.experimental.pallas import tpu as pltpu
from jax.sharding import PartitionSpec as P

NT = (((1,), (1,)), ((), ()))
TN = (((0,), (0,)), ((), ()))
VMEM = pl.BlockSpec(memory_space=pltpu.VMEM)
SMEM = pl.BlockSpec(memory_space=pltpu.SMEM)
HBM = pl.BlockSpec(memory_space=pl.ANY)


def here(x):
    return pltpu.with_memory_space_constraint(x, pltpu.VMEM)


def far(x):
    return pltpu.with_memory_space_constraint(x, pltpu.HBM)


def matrix_at(owner, slot):
    matrix = jnp.int32(0)
    for m in range(owner.shape[0]):
        matrix = jnp.where(owner[m] == slot, m, matrix)
    return matrix


def slot_rows(in_v, other_v, out_v, matrix, lengths, tiles, store):
    seqs, _, width, length = out_v.shape
    rows = 2 * in_v.shape[2]
    stride = tiles.shape[0] // seqs
    per = length // width
    scale = length ** (-0.5)
    lane = lax.broadcasted_iota(jnp.int32, (1, length), 1)
    for s in range(seqs):
        left = jnp.concatenate([in_v[s, matrix], other_v[s, matrix]], axis=0)
        left = jnp.where(lane < lengths[s], left, 0)
        tile = lax.dot_general(left, out_v[s, matrix], NT, preferred_element_type=jnp.float32)
        tiles[s * stride:s * stride + rows, :] = jnp.concatenate([tile] * per, axis=1)
    for t in range(rows // per):
        tile = tiles[pl.ds(per * t, seqs, stride=stride), :]
        for p in range(1, per):
            other = tiles[pl.ds(per * t + p, seqs, stride=stride), :]
            tile = jnp.where(lane < p * width, tile, other)
        store(t * length, (tile * scale).astype(jnp.bfloat16))


def load_body(*refs):
    *refs, through, sem, out_sem = refs
    n = len(refs) // 2
    parts = sem.shape[1]

    def copies(source, target, sems):
        each = source.shape[0] // parts
        return [
            pltpu.make_async_copy(source.at[pl.ds(j * each, each)], target.at[pl.ds(j * each, each)], sems.at[j])
            for j in range(parts)
        ]

    inward = copies(refs[n - 1], through, sem.at[n - 1])
    outward = copies(through, refs[2 * n - 1], out_sem)
    near = [copies(refs[i], refs[n + i], sem.at[i]) for i in range(n - 1)]
    for copy in inward + sum(near, []):
        copy.start()
    for one, two in zip(inward, outward):
        one.wait()
        two.start()
    for copy in sum(near, []) + outward:
        copy.wait()


def load(near, distant):
    arrays = (*near, distant)
    parts = 4 if distant.shape[0] % 64 == 0 and all(a.shape[0] % 4 == 0 for a in near) else 1
    return pl.pallas_call(
        load_body,
        out_shape=[pltpu.VMEM(a.shape, a.dtype) for a in near] + [pltpu.HBM(distant.shape, distant.dtype)],
        in_specs=[HBM] * len(arrays),
        out_specs=[VMEM] * len(near) + [HBM],
        scratch_shapes=[
            pltpu.VMEM(distant.shape, distant.dtype),
            pltpu.SemaphoreType.DMA((len(arrays), parts)),
            pltpu.SemaphoreType.DMA((parts,)),
        ],
        compiler_params=pltpu.CompilerParams(vmem_limit_bytes=4 << 20),
        name="load",
    )(*[far(a) for a in arrays])


def whole_body(pairs, owner, me, core, lengths, in_v, other_v, out_v, _, *refs):
    grads, tiles = refs[:len(pairs)], refs[-1]
    half = grads[0].shape[1] // 2
    for at, pair in enumerate(pairs):
        matrix = matrix_at(owner, me[0] ^ jnp.where(core[0] == 0, pair[0], pair[1]))

        def store(column, x):
            first = jnp.where(core[0] == 0, column, (column + half) % (2 * half))
            grads[at][:, pl.ds(pl.multiple_of(first, 128), x.shape[1])] = x

        slot_rows(in_v, other_v, out_v, matrix, lengths, tiles.at[at % 2], store)


def whole_slots(pairs, owner, me, core, lengths, in_v, other_in, out_v, passed):
    seqs, _, rows, length = in_v.shape
    width = out_v.shape[2]
    n = len(pairs)
    return pl.pallas_call(
        functools.partial(whole_body, pairs),
        out_shape=[pltpu.VMEM((seqs, 2 * rows * width), jnp.bfloat16)] * n
        + [pltpu.HBM(passed.shape, passed.dtype)],
        in_specs=[SMEM] * 4 + [VMEM] * 3 + [HBM],
        out_specs=[VMEM] * n + [HBM],
        input_output_aliases={7: n},
        scratch_shapes=[pltpu.VMEM((2, seqs * (2 * rows + 8), length), jnp.float32)],
        compiler_params=pltpu.CompilerParams(vmem_limit_bytes=12 << 20),
        cost_estimate=pl.CostEstimate(
            flops=4 * n * seqs * rows * width * length,
            bytes_accessed=2 * n * seqs * length * (2 * rows + width),
            transcendentals=0,
        ),
        name="whole_slots",
    )(far(owner), me, core, far(lengths), here(in_v), here(other_in), here(out_v), far(passed))


def score_body(pairs, rows_each, cores, core, me, ids, *refs):
    mine, theirs = refs[:len(pairs)], refs[len(pairs):2 * len(pairs)]
    own_q, other_q, s_ref, x_ref = refs[2 * len(pairs):]
    seqs, width = mine[0].shape
    half = width // 2
    rows = s_ref.shape[0]
    total = ids.shape[1]
    own_at = pl.ds(pl.multiple_of(core[0] * half, 128), half)
    other_at = pl.ds(pl.multiple_of((1 - core[0]) * half, 128), half)

    def place(k):
        return pl.ds(pl.multiple_of((me[0] ^ k) * seqs, 16), seqs)

    for pair, own, other in zip(pairs, mine, theirs):
        x_ref[place(jnp.where(core[0] == 0, pair[0], pair[1])), :] = own[...]
        x_ref[place(jnp.where(core[0] == 0, pair[1], pair[0])), :] = other[...]
    at = lax.broadcasted_iota(jnp.int32, (rows, total), 0)
    wanted = (at // rows_each * cores + core[0]) * rows_each + at % rows_each
    pick = jnp.where(wanted == ids[...], 1.0, 0.0).astype(jnp.bfloat16)
    for first, where, q_ref in ((True, own_at, own_q), (False, other_at, other_q)):
        picked = jnp.dot(pick, x_ref[:, where], preferred_element_type=jnp.float32).astype(jnp.bfloat16)
        part = lax.dot_general(picked, q_ref[...], NT, preferred_element_type=jnp.float32)
        s_ref[...] = part if first else s_ref[...] + part


def partial_scores(pairs, core, me, ids, mine, theirs, own_q, other_q):
    cores = 2
    seqs, width = mine[0].shape
    half = width // 2
    total = ids.shape[1]
    queries = own_q.shape[0]
    rows = total // cores
    rows_each = rows // (total // seqs)
    args = [*mine, *theirs, own_q, other_q]
    return pl.pallas_call(
        functools.partial(score_body, pairs, rows_each, cores),
        out_shape=[pltpu.VMEM((rows, queries), jnp.float32), pltpu.VMEM((total, 2 * half), jnp.bfloat16)],
        in_specs=[SMEM, SMEM] + [VMEM] * (1 + len(args)),
        out_specs=[VMEM] * 2,
        compiler_params=pltpu.CompilerParams(vmem_limit_bytes=16 << 20),
        cost_estimate=pl.CostEstimate(
            flops=4 * rows * queries * half, bytes_accessed=4 * half * (queries + total), transcendentals=0
        ),
        name="scores",
    )(core, me, ids, *[here(arg) for arg in args])


def fisher_body(total, core, x_ref, f_hbm, left, out, sem):
    half = x_ref.shape[1] // 2
    depth, block, _ = out.shape
    step = 512 if half % 512 == 0 else half
    for at in range(0, half, block):
        where = pl.ds(pl.multiple_of(core[0] * half + at, 128), block)
        left[at:at + block, :] = x_ref[:, where].T

    def copy(i):
        rows = pl.ds(pl.multiple_of(i * block, block), block)
        return pltpu.make_async_copy(out.at[i % depth], f_hbm.at[0, rows], sem.at[i % depth])

    @pl.loop(0, half // block)
    def _(i):
        @pl.when(i >= depth)
        def _():
            copy(i - depth).wait()

        rows = left[pl.ds(pl.multiple_of(i * block, block), block), :]
        for at in range(0, 2 * half, step):
            tile = jnp.dot(rows, x_ref[:, at:at + step], preferred_element_type=jnp.float32)
            out[i % depth, :, at:at + step] = (tile * (1.0 / total)).astype(out.dtype)
        copy(i).start()

    for i in range(half // block - depth, half // block):
        copy(i).wait()


def fisher_block(core, x):
    total, half = x.shape[0], x.shape[1] // 2
    block, depth = (256, 4) if half % 256 == 0 and half >= 1024 else (half, 1)
    return pl.pallas_call(
        functools.partial(fisher_body, total),
        out_shape=jax.ShapeDtypeStruct((1, half, 2 * half), jnp.bfloat16),
        in_specs=[SMEM, VMEM],
        out_specs=HBM,
        scratch_shapes=[
            pltpu.VMEM((half, total), jnp.bfloat16),
            pltpu.VMEM((depth, block, 2 * half), jnp.bfloat16),
            pltpu.SemaphoreType.DMA((depth,)),
        ],
        compiler_params=pltpu.CompilerParams(vmem_limit_bytes=24 << 20),
        cost_estimate=pl.CostEstimate(
            flops=4 * total * half * half, bytes_accessed=4 * half * (half + total), transcendentals=0
        ),
        name="fisher",
    )(core, here(x))


def local(dp, cores, in_factor, out_factor, seq_lengths, sequence_ids, matrix_owner, queries):
    assert cores == 2 and dp % 2 == 0 and dp & (dp - 1) == 0
    swap = [(0, 1), (1, 0)]
    core = lax.axis_index("mat").astype(jnp.int32)[None]
    me = lax.axis_index("dp").astype(jnp.int32)[None]
    other_in = lax.ppermute(in_factor, "mat", swap)
    own_q = queries[0]
    in_v, out_v, late_q = load((in_factor, out_factor), own_q)
    order = list(range(dp // 2, dp)) + list(range(1, dp // 2)) + [0]
    pairs = tuple(zip(order[::2], order[1::2]))
    *made, late_q = whole_slots(pairs, matrix_owner, me, core, seq_lengths, in_v, other_in, out_v, late_q)
    mine = [
        lax.ppermute(
            piece, ("dp", "mat"), [(d * 2 + c, (d ^ pair[c]) * 2 + c) for d in range(dp) for c in range(2)]
        )
        for pair, piece in zip(pairs, made)
    ]
    other_q = lax.ppermute(late_q, "mat", swap)
    theirs = [lax.ppermute(piece, "mat", swap) for piece in mine]
    part, x = partial_scores(pairs, core, me, sequence_ids[None, :], mine, theirs, own_q, other_q)
    parts = lax.all_to_all(
        part.reshape(dp, part.shape[0] // dp, -1), "dp", split_axis=0, concat_axis=0, tiled=True
    )
    fisher = fisher_block(core, x)
    return (fisher, jnp.sum(parts, axis=0))


def solution(mesh):
    in_specs = (
        P(("groups", "dp"), None, "mat", None),
        P(("groups", "dp"), None, None, None),
        P(("groups", "dp")),
        P("groups"),
        P(),
        P("dp", None, "mat"),
    )
    out_specs = (P(("groups", "dp"), "mat", None), P(("groups", "dp", "mat"), None))
    body = functools.partial(local, mesh.shape["dp"], mesh.shape["mat"])
    return jax.shard_map(body, mesh=mesh, in_specs=in_specs, out_specs=out_specs, check_vma=False)
```

```python
import functools

import jax
import jax.numpy as jnp
from jax import lax
from jax.experimental import pallas as pl
from jax.experimental.pallas import tpu as pltpu
from jax.sharding import PartitionSpec as P

NT = (((1,), (1,)), ((), ()))
TN = (((0,), (0,)), ((), ()))
VMEM = pl.BlockSpec(memory_space=pltpu.VMEM)
SMEM = pl.BlockSpec(memory_space=pltpu.SMEM)
HBM = pl.BlockSpec(memory_space=pl.ANY)


def here(x):
    return pltpu.with_memory_space_constraint(x, pltpu.VMEM)


def scalars(x):
    return pltpu.with_memory_space_constraint(x, pltpu.SMEM)


def far(x):
    return pltpu.with_memory_space_constraint(x, pltpu.HBM)


def matrix_at(owner, slot):
    matrix = jnp.int32(0)
    for m in range(owner.shape[0]):
        matrix = jnp.where(owner[m] == slot, m, matrix)
    return matrix


def slot_rows(in_v, other_v, out_v, matrix, length_of, tiles, store):
    seqs, _, width, length = out_v.shape
    rows = 2 * in_v.shape[2]
    stride = tiles.shape[0] // seqs
    per = length // width
    scale = length ** (-0.5)
    lane = lax.broadcasted_iota(jnp.int32, (1, length), 1)
    for s in range(seqs):
        left = jnp.concatenate([in_v[s, matrix], other_v[s, matrix]], axis=0)
        left = jnp.where(lane < length_of(s), left, 0)
        tile = lax.dot_general(left, out_v[s, matrix], NT, preferred_element_type=jnp.float32)
        tiles[s * stride:s * stride + rows, :] = jnp.concatenate([tile] * per, axis=1)
    for t in range(rows // per):
        tile = tiles[pl.ds(per * t, seqs, stride=stride), :]
        for p in range(1, per):
            other = tiles[pl.ds(per * t + p, seqs, stride=stride), :]
            tile = jnp.where(lane < p * width, tile, other)
        store(t * length, (tile * scale).astype(jnp.bfloat16))


def load_body(pairs, owner_hbm, lengths_hbm, *refs):
    *refs, facts, owner, lengths, sem, small = refs
    n = len(refs) // 2
    parts = sem.shape[1]
    copies = []
    for i in range(n):
        each = refs[i].shape[0] // parts
        for j in range(parts):
            part = pl.ds(j * each, each)
            copies.append(pltpu.make_async_copy(refs[i].at[part], refs[n + i].at[part], sem.at[i, j]))
    scalar_copies = [
        pltpu.make_async_copy(owner_hbm, owner, small.at[0]),
        pltpu.make_async_copy(lengths_hbm, lengths, small.at[1]),
    ]
    for copy in scalar_copies + copies:
        copy.start()
    core, me = lax.axis_index("mat"), lax.axis_index("dp")
    facts[0] = core
    facts[1] = me
    for copy in scalar_copies:
        copy.wait()
    for at, pair in enumerate(pairs):
        facts[2 + at] = matrix_at(owner, me ^ jnp.where(core == 0, pair[0], pair[1]))
    for s in range(lengths.shape[0]):
        facts[2 + len(pairs) + s] = lengths[s]
    for copy in copies:
        copy.wait()


def load(pairs, owner, lengths, *arrays):
    parts = 4 if all(a.shape[0] % 4 == 0 for a in arrays) else 1
    return pl.pallas_call(
        functools.partial(load_body, pairs),
        out_shape=[pltpu.VMEM(a.shape, a.dtype) for a in arrays]
        + [pltpu.SMEM((2 + len(pairs) + lengths.shape[0],), jnp.int32)],
        in_specs=[HBM] * (2 + len(arrays)),
        out_specs=[VMEM] * len(arrays) + [SMEM],
        scratch_shapes=[
            pltpu.SMEM(owner.shape, jnp.int32),
            pltpu.SMEM(lengths.shape, jnp.int32),
            pltpu.SemaphoreType.DMA((len(arrays), parts)),
            pltpu.SemaphoreType.DMA((2,)),
        ],
        compiler_params=pltpu.CompilerParams(vmem_limit_bytes=4 << 20),
        name="load",
    )(far(owner), far(lengths), *[far(a) for a in arrays])


def whole_body(n, facts, in_v, other_v, out_v, _, *refs):
    grads, tiles = refs[:n], refs[-1]
    half = grads[0].shape[1] // 2
    for at in range(n):

        def store(column, x):
            first = jnp.where(facts[0] == 0, column, (column + half) % (2 * half))
            grads[at][:, pl.ds(pl.multiple_of(first, 128), x.shape[1])] = x

        slot_rows(in_v, other_v, out_v, facts[2 + at], lambda s: facts[2 + n + s], tiles.at[at % 2], store)


def whole_slots(n, facts, in_v, other_in, out_v, passed):
    seqs, _, rows, length = in_v.shape
    width = out_v.shape[2]
    return pl.pallas_call(
        functools.partial(whole_body, n),
        out_shape=[pltpu.VMEM((seqs, 2 * rows * width), jnp.bfloat16)] * n
        + [pltpu.VMEM(passed.shape, passed.dtype)],
        in_specs=[SMEM] + [VMEM] * 4,
        out_specs=[VMEM] * (n + 1),
        input_output_aliases={4: n},
        scratch_shapes=[pltpu.VMEM((2, seqs * (2 * rows + 8), length), jnp.float32)],
        compiler_params=pltpu.CompilerParams(vmem_limit_bytes=12 << 20),
        cost_estimate=pl.CostEstimate(
            flops=4 * n * seqs * rows * width * length,
            bytes_accessed=2 * n * seqs * length * (2 * rows + width),
            transcendentals=0,
        ),
        name="whole_slots",
    )(scalars(facts), here(in_v), here(other_in), here(out_v), here(passed))


def score_body(pairs, rows_each, cores, facts, ids, *refs):
    core, me = facts[0], facts[1]
    mine, theirs = refs[:len(pairs)], refs[len(pairs):2 * len(pairs)]
    own_q, other_q, s_ref, x_ref = refs[2 * len(pairs):]
    seqs, width = mine[0].shape
    half = width // 2
    rows = s_ref.shape[0]
    total = ids.shape[1]
    own_at = pl.ds(pl.multiple_of(core * half, 128), half)
    other_at = pl.ds(pl.multiple_of((1 - core) * half, 128), half)

    def place(k):
        return pl.ds(pl.multiple_of((me ^ k) * seqs, 16), seqs)

    for pair, own, other in zip(pairs, mine, theirs):
        x_ref[place(jnp.where(core == 0, pair[0], pair[1])), :] = own[...]
        x_ref[place(jnp.where(core == 0, pair[1], pair[0])), :] = other[...]
    at = lax.broadcasted_iota(jnp.int32, (rows, total), 0)
    wanted = (at // rows_each * cores + core) * rows_each + at % rows_each
    pick = jnp.where(wanted == ids[...], 1.0, 0.0).astype(jnp.bfloat16)
    for first, where, q_ref in ((True, own_at, own_q), (False, other_at, other_q)):
        picked = jnp.dot(pick, x_ref[:, where], preferred_element_type=jnp.float32).astype(jnp.bfloat16)
        part = lax.dot_general(picked, q_ref[...], NT, preferred_element_type=jnp.float32)
        s_ref[...] = part if first else s_ref[...] + part


def partial_scores(pairs, facts, ids, mine, theirs, own_q, other_q):
    cores = 2
    seqs, width = mine[0].shape
    half = width // 2
    total = ids.shape[1]
    queries = own_q.shape[0]
    rows = total // cores
    rows_each = rows // (total // seqs)
    args = [*mine, *theirs, own_q, other_q]
    return pl.pallas_call(
        functools.partial(score_body, pairs, rows_each, cores),
        out_shape=[pltpu.VMEM((rows, queries), jnp.float32), pltpu.VMEM((total, 2 * half), jnp.bfloat16)],
        in_specs=[SMEM] + [VMEM] * (1 + len(args)),
        out_specs=[VMEM] * 2,
        compiler_params=pltpu.CompilerParams(vmem_limit_bytes=16 << 20),
        cost_estimate=pl.CostEstimate(
            flops=4 * rows * queries * half, bytes_accessed=4 * half * (queries + total), transcendentals=0
        ),
        name="scores",
    )(scalars(facts), ids, *[here(arg) for arg in args])


def fisher_body(total, facts, x_ref, f_hbm, left, out, sem):
    half = x_ref.shape[1] // 2
    depth, block, _ = out.shape
    step = 512 if half % 512 == 0 else half
    for at in range(0, half, block):
        where = pl.ds(pl.multiple_of(facts[0] * half + at, 128), block)
        left[at:at + block, :] = x_ref[:, where].T

    def copy(i):
        rows = pl.ds(pl.multiple_of(i * block, block), block)
        return pltpu.make_async_copy(out.at[i % depth], f_hbm.at[0, rows], sem.at[i % depth])

    @pl.loop(0, half // block)
    def _(i):
        @pl.when(i >= depth)
        def _():
            copy(i - depth).wait()

        rows = left[pl.ds(pl.multiple_of(i * block, block), block), :]
        for at in range(0, 2 * half, step):
            tile = jnp.dot(rows, x_ref[:, at:at + step], preferred_element_type=jnp.float32)
            out[i % depth, :, at:at + step] = (tile * (1.0 / total)).astype(out.dtype)
        copy(i).start()

    for i in range(half // block - depth, half // block):
        copy(i).wait()


def fisher_block(facts, x):
    total, half = x.shape[0], x.shape[1] // 2
    block, depth = (256, 4) if half % 256 == 0 and half >= 1024 else (half, 1)
    return pl.pallas_call(
        functools.partial(fisher_body, total),
        out_shape=jax.ShapeDtypeStruct((1, half, 2 * half), jnp.bfloat16),
        in_specs=[SMEM, VMEM],
        out_specs=HBM,
        scratch_shapes=[
            pltpu.VMEM((half, total), jnp.bfloat16),
            pltpu.VMEM((depth, block, 2 * half), jnp.bfloat16),
            pltpu.SemaphoreType.DMA((depth,)),
        ],
        compiler_params=pltpu.CompilerParams(vmem_limit_bytes=24 << 20),
        cost_estimate=pl.CostEstimate(
            flops=4 * total * half * half, bytes_accessed=4 * half * (half + total), transcendentals=0
        ),
        name="fisher",
    )(scalars(facts), here(x))


def local(dp, cores, in_factor, out_factor, seq_lengths, sequence_ids, matrix_owner, queries):
    assert cores == 2 and dp % 2 == 0 and dp & (dp - 1) == 0
    swap = [(0, 1), (1, 0)]
    order = list(range(dp // 2, dp)) + list(range(1, dp // 2)) + [0]
    pairs = tuple(zip(order[::2], order[1::2]))
    other_in = lax.ppermute(in_factor, "mat", swap)
    in_v, out_v, own_q, facts = load(
        pairs, matrix_owner, seq_lengths, in_factor, out_factor, queries[0]
    )
    *made, own_q = whole_slots(len(pairs), facts, in_v, other_in, out_v, own_q)
    mine = [
        lax.ppermute(
            piece, ("dp", "mat"), [(d * 2 + c, (d ^ pair[c]) * 2 + c) for d in range(dp) for c in range(2)]
        )
        for pair, piece in zip(pairs, made)
    ]
    other_q = lax.ppermute(own_q, "mat", swap)
    theirs = [lax.ppermute(piece, "mat", swap) for piece in mine]
    part, x = partial_scores(pairs, facts, sequence_ids[None, :], mine, theirs, own_q, other_q)
    parts = lax.all_to_all(
        part.reshape(dp, part.shape[0] // dp, -1), "dp", split_axis=0, concat_axis=0, tiled=True
    )
    fisher = fisher_block(facts, x)
    return (fisher, jnp.sum(parts, axis=0))


def solution(mesh):
    in_specs = (
        P(("groups", "dp"), None, "mat", None),
        P(("groups", "dp"), None, None, None),
        P(("groups", "dp")),
        P("groups"),
        P(),
        P("dp", None, "mat"),
    )
    out_specs = (P(("groups", "dp"), "mat", None), P(("groups", "dp", "mat"), None))
    body = functools.partial(local, mesh.shape["dp"], mesh.shape["mat"])
    return jax.shard_map(body, mesh=mesh, in_specs=in_specs, out_specs=out_specs, check_vma=False)
```

```python
import functools

import jax
import jax.numpy as jnp
from jax import lax
from jax.experimental import pallas as pl
from jax.experimental.pallas import tpu as pltpu
from jax.sharding import PartitionSpec as P

NT = (((1,), (1,)), ((), ()))
TN = (((0,), (0,)), ((), ()))
VMEM = pl.BlockSpec(memory_space=pltpu.VMEM)
SMEM = pl.BlockSpec(memory_space=pltpu.SMEM)
HBM = pl.BlockSpec(memory_space=pl.ANY)


def here(x):
    return pltpu.with_memory_space_constraint(x, pltpu.VMEM)


def scalars(x):
    return pltpu.with_memory_space_constraint(x, pltpu.SMEM)


def far(x):
    return pltpu.with_memory_space_constraint(x, pltpu.HBM)


def matrix_at(owner, slot):
    matrix = jnp.int32(0)
    for m in range(owner.shape[0]):
        matrix = jnp.where(owner[m] == slot, m, matrix)
    return matrix


def slot_rows(in_v, other_v, out_v, matrix, length_of, tiles, store):
    seqs, _, width, length = out_v.shape
    rows = 2 * in_v.shape[2]
    stride = tiles.shape[0] // seqs
    per = length // width
    scale = length ** (-0.5)
    lane = lax.broadcasted_iota(jnp.int32, (1, length), 1)
    for s in range(seqs):
        left = jnp.concatenate([in_v[s, matrix], other_v[s, matrix]], axis=0)
        left = jnp.where(lane < length_of(s), left, 0)
        tile = lax.dot_general(left, out_v[s, matrix], NT, preferred_element_type=jnp.float32)
        tiles[s * stride:s * stride + rows, :] = jnp.concatenate([tile] * per, axis=1)
    for t in range(rows // per):
        tile = tiles[pl.ds(per * t, seqs, stride=stride), :]
        for p in range(1, per):
            other = tiles[pl.ds(per * t + p, seqs, stride=stride), :]
            tile = jnp.where(lane < p * width, tile, other)
        store(t * length, (tile * scale).astype(jnp.bfloat16))


def load_body(pairs, owner_hbm, lengths_hbm, *refs):
    *refs, facts, owner, lengths, sem, small = refs
    n = len(refs) // 2
    parts = sem.shape[1]
    copies = []
    for i in range(n):
        each = refs[i].shape[0] // parts
        for j in range(parts):
            part = pl.ds(j * each, each)
            copies.append(pltpu.make_async_copy(refs[i].at[part], refs[n + i].at[part], sem.at[i, j]))
    scalar_copies = [
        pltpu.make_async_copy(owner_hbm, owner, small.at[0]),
        pltpu.make_async_copy(lengths_hbm, lengths, small.at[1]),
    ]
    for copy in scalar_copies + copies:
        copy.start()
    core, me = lax.axis_index("mat"), lax.axis_index("dp")
    facts[0] = core
    facts[1] = me
    for copy in scalar_copies:
        copy.wait()
    for at, pair in enumerate(pairs):
        facts[2 + at] = matrix_at(owner, me ^ jnp.where(core == 0, pair[0], pair[1]))
    for s in range(lengths.shape[0]):
        facts[2 + len(pairs) + s] = lengths[s]
    for copy in copies:
        copy.wait()


def load(pairs, owner, lengths, *arrays):
    parts = 4 if all(a.shape[0] % 4 == 0 for a in arrays) else 1
    return pl.pallas_call(
        functools.partial(load_body, pairs),
        out_shape=[pltpu.VMEM(a.shape, a.dtype) for a in arrays]
        + [pltpu.SMEM((2 + len(pairs) + lengths.shape[0],), jnp.int32)],
        in_specs=[HBM] * (2 + len(arrays)),
        out_specs=[VMEM] * len(arrays) + [SMEM],
        scratch_shapes=[
            pltpu.SMEM(owner.shape, jnp.int32),
            pltpu.SMEM(lengths.shape, jnp.int32),
            pltpu.SemaphoreType.DMA((len(arrays), parts)),
            pltpu.SemaphoreType.DMA((2,)),
        ],
        compiler_params=pltpu.CompilerParams(vmem_limit_bytes=4 << 20),
        name="load",
    )(far(owner), far(lengths), *[far(a) for a in arrays])


def whole_body(n, facts, in_v, other_v, out_v, _, *refs):
    grads, tiles = refs[:n], refs[-1]
    half = grads[0].shape[1] // 2
    for at in range(n):

        def store(column, x):
            first = jnp.where(facts[0] == 0, column, (column + half) % (2 * half))
            grads[at][:, pl.ds(pl.multiple_of(first, 128), x.shape[1])] = x

        slot_rows(in_v, other_v, out_v, facts[2 + at], lambda s: facts[2 + n + s], tiles.at[at % 2], store)


def whole_slots(n, facts, in_v, other_in, out_v, passed):
    seqs, _, rows, length = in_v.shape
    width = out_v.shape[2]
    return pl.pallas_call(
        functools.partial(whole_body, n),
        out_shape=[pltpu.VMEM((seqs, 2 * rows * width), jnp.bfloat16)] * n
        + [pltpu.VMEM(passed.shape, passed.dtype)],
        in_specs=[SMEM] + [VMEM] * 4,
        out_specs=[VMEM] * (n + 1),
        input_output_aliases={4: n},
        scratch_shapes=[pltpu.VMEM((2, seqs * (2 * rows + 8), length), jnp.float32)],
        compiler_params=pltpu.CompilerParams(vmem_limit_bytes=12 << 20),
        cost_estimate=pl.CostEstimate(
            flops=4 * n * seqs * rows * width * length,
            bytes_accessed=2 * n * seqs * length * (2 * rows + width),
            transcendentals=0,
        ),
        name="whole_slots",
    )(scalars(facts), here(in_v), here(other_in), here(out_v), here(passed))


def score_body(pairs, facts, ids, *refs):
    n = len(pairs)
    pieces, (own_q, other_q, s_ref, x, t) = refs[:n], refs[n:]
    core, me = facts[0], facts[1]
    seqs, width = pieces[0].shape
    half = width // 2
    total = ids.shape[1]
    own_at = pl.ds(pl.multiple_of(core * half, 128), half)
    other_at = pl.ds(pl.multiple_of((1 - core) * half, 128), half)
    for at, piece in enumerate(pieces):
        x[at * seqs:(at + 1) * seqs, :] = piece[...]
    part = lax.dot_general(x[:, own_at], own_q[...], NT, preferred_element_type=jnp.float32)
    part += lax.dot_general(x[:, other_at], other_q[...], NT, preferred_element_type=jnp.float32)
    t[...] = jnp.zeros_like(t)
    for at, pair in enumerate(pairs):
        rows = (me ^ jnp.where(core == 0, pair[0], pair[1])) * seqs
        t[pl.ds(pl.multiple_of(rows, 16), seqs), :] = part[at * seqs:(at + 1) * seqs].astype(t.dtype)
    wanted = lax.broadcasted_iota(jnp.int32, (total, total), 0)
    pick = jnp.where(wanted == ids[...], 1.0, 0.0).astype(t.dtype)
    s_ref[...] = jnp.dot(pick, t[...], preferred_element_type=jnp.float32).astype(s_ref.dtype)


def partial_scores(pairs, facts, ids, pieces, own_q, other_q):
    seqs, width = pieces[0].shape
    total = ids.shape[1]
    queries = own_q.shape[0]
    args = [*pieces, own_q, other_q]
    rows = len(pairs) * seqs
    return pl.pallas_call(
        functools.partial(score_body, pairs),
        out_shape=jax.ShapeDtypeStruct((total, queries), jnp.bfloat16),
        in_specs=[SMEM] + [VMEM] * (1 + len(args)),
        out_specs=VMEM,
        scratch_shapes=[pltpu.VMEM((rows, width), jnp.bfloat16), pltpu.VMEM((total, queries), jnp.bfloat16)],
        compiler_params=pltpu.CompilerParams(vmem_limit_bytes=16 << 20),
        cost_estimate=pl.CostEstimate(
            flops=2 * rows * queries * width, bytes_accessed=2 * width * (queries + rows), transcendentals=0
        ),
        name="scores",
    )(scalars(facts), ids, *[here(arg) for arg in args])


def fisher_body(total, facts, *refs):
    *pieces, f_hbm, x_ref, left, out, sem = refs
    seqs = pieces[0].shape[0]
    for at, piece in enumerate(pieces):
        x_ref[at * seqs:(at + 1) * seqs, :] = piece[...]
    half = x_ref.shape[1] // 2
    depth, block, _ = out.shape
    step = 512 if half % 512 == 0 else half
    for at in range(0, half, block):
        where = pl.ds(pl.multiple_of(facts[0] * half + at, 128), block)
        left[at:at + block, :] = x_ref[:, where].T

    def copy(i):
        rows = pl.ds(pl.multiple_of(i * block, block), block)
        return pltpu.make_async_copy(out.at[i % depth], f_hbm.at[0, rows], sem.at[i % depth])

    @pl.loop(0, half // block)
    def _(i):
        @pl.when(i >= depth)
        def _():
            copy(i - depth).wait()

        rows = left[pl.ds(pl.multiple_of(i * block, block), block), :]
        for at in range(0, 2 * half, step):
            tile = jnp.dot(rows, x_ref[:, at:at + step], preferred_element_type=jnp.float32)
            out[i % depth, :, at:at + step] = (tile * (1.0 / total)).astype(out.dtype)
        copy(i).start()

    for i in range(half // block - depth, half // block):
        copy(i).wait()


def fisher_block(facts, pieces):
    seqs, width = pieces[0].shape
    total, half = len(pieces) * seqs, width // 2
    block, depth = (256, 4) if half % 256 == 0 and half >= 1024 else (half, 1)
    return pl.pallas_call(
        functools.partial(fisher_body, total),
        out_shape=jax.ShapeDtypeStruct((1, half, 2 * half), jnp.bfloat16),
        in_specs=[SMEM] + [VMEM] * len(pieces),
        out_specs=HBM,
        scratch_shapes=[
            pltpu.VMEM((total, width), jnp.bfloat16),
            pltpu.VMEM((half, total), jnp.bfloat16),
            pltpu.VMEM((depth, block, 2 * half), jnp.bfloat16),
            pltpu.SemaphoreType.DMA((depth,)),
        ],
        compiler_params=pltpu.CompilerParams(vmem_limit_bytes=24 << 20),
        cost_estimate=pl.CostEstimate(
            flops=4 * total * half * half, bytes_accessed=4 * half * (half + total), transcendentals=0
        ),
        name="fisher",
    )(scalars(facts), *[here(piece) for piece in pieces])


def local(dp, cores, in_factor, out_factor, seq_lengths, sequence_ids, matrix_owner, queries):
    assert cores == 2 and dp % 4 == 0 and dp & (dp - 1) == 0
    swap = [(0, 1), (1, 0)]
    distant, near = range(dp // 2, dp), range(dp // 2 - 1, -1, -1)
    pairs = []
    for at in range(0, dp // 2, 2):
        pairs += [(distant[at], distant[at + 1]), (near[at], near[at + 1])]
    pairs = tuple(pairs)
    other_in = lax.ppermute(in_factor, "mat", swap)
    in_v, out_v, own_q, facts = load(
        pairs, matrix_owner, seq_lengths, in_factor, out_factor, queries[0]
    )
    *made, own_q = whole_slots(len(pairs), facts, in_v, other_in, out_v, own_q)
    mine = [
        lax.ppermute(
            piece, ("dp", "mat"), [(d * 2 + c, (d ^ pair[c]) * 2 + c) for d in range(dp) for c in range(2)]
        )
        for pair, piece in zip(pairs, made)
    ]
    other_q = lax.ppermute(own_q, "mat", swap)
    theirs = [lax.ppermute(piece, "mat", swap) for piece in mine]
    part = partial_scores(pairs, facts, sequence_ids[None, :], mine, own_q, other_q)
    parts = lax.all_to_all(
        part.reshape(dp * cores, part.shape[0] // (dp * cores), -1),
        ("dp", "mat"),
        split_axis=0,
        concat_axis=0,
        tiled=True,
    )
    fisher = fisher_block(facts, mine + theirs)
    return (fisher, jnp.sum(parts.astype(jnp.float32), axis=0))


def solution(mesh):
    in_specs = (
        P(("groups", "dp"), None, "mat", None),
        P(("groups", "dp"), None, None, None),
        P(("groups", "dp")),
        P("groups"),
        P(),
        P("dp", None, "mat"),
    )
    out_specs = (P(("groups", "dp"), "mat", None), P(("groups", "dp", "mat"), None))
    body = functools.partial(local, mesh.shape["dp"], mesh.shape["mat"])
    return jax.shard_map(body, mesh=mesh, in_specs=in_specs, out_specs=out_specs, check_vma=False)
```

```python
import functools

import jax
import jax.numpy as jnp
from jax import lax
from jax.experimental import pallas as pl
from jax.experimental.pallas import tpu as pltpu
from jax.sharding import PartitionSpec as P

NT = (((1,), (1,)), ((), ()))
TN = (((0,), (0,)), ((), ()))
VMEM = pl.BlockSpec(memory_space=pltpu.VMEM)
SMEM = pl.BlockSpec(memory_space=pltpu.SMEM)
HBM = pl.BlockSpec(memory_space=pl.ANY)


def here(x):
    return pltpu.with_memory_space_constraint(x, pltpu.VMEM)


def scalars(x):
    return pltpu.with_memory_space_constraint(x, pltpu.SMEM)


def far(x):
    return pltpu.with_memory_space_constraint(x, pltpu.HBM)


def matrix_at(owner, slot):
    matrix = jnp.int32(0)
    for m in range(owner.shape[0]):
        matrix = jnp.where(owner[m] == slot, m, matrix)
    return matrix


def slot_rows(in_v, other_v, out_v, matrix, length_of, tiles, store):
    seqs, _, width, length = out_v.shape
    rows = 2 * in_v.shape[2]
    stride = tiles.shape[0] // seqs
    per = length // width
    scale = length ** (-0.5)
    lane = lax.broadcasted_iota(jnp.int32, (1, length), 1)
    for s in range(seqs):
        left = jnp.concatenate([in_v[s, matrix], other_v[s, matrix]], axis=0)
        left = jnp.where(lane < length_of(s), left, 0)
        tile = lax.dot_general(left, out_v[s, matrix], NT, preferred_element_type=jnp.float32)
        tiles[s * stride:s * stride + rows, :] = jnp.concatenate([tile] * per, axis=1)
    for t in range(rows // per):
        tile = tiles[pl.ds(per * t, seqs, stride=stride), :]
        for p in range(1, per):
            other = tiles[pl.ds(per * t + p, seqs, stride=stride), :]
            tile = jnp.where(lane < p * width, tile, other)
        store(t * length, (tile * scale).astype(jnp.bfloat16))


def load_body(pairs, owner_hbm, lengths_hbm, *refs):
    *refs, facts, owner, lengths, sem, small = refs
    n = len(refs) // 2
    parts = sem.shape[1]
    copies = []
    for i in range(n):
        each = refs[i].shape[0] // parts
        for j in range(parts):
            part = pl.ds(j * each, each)
            copies.append(pltpu.make_async_copy(refs[i].at[part], refs[n + i].at[part], sem.at[i, j]))
    scalar_copies = [
        pltpu.make_async_copy(owner_hbm, owner, small.at[0]),
        pltpu.make_async_copy(lengths_hbm, lengths, small.at[1]),
    ]
    for copy in scalar_copies + copies:
        copy.start()
    core, me = lax.axis_index("mat"), lax.axis_index("dp")
    facts[0] = core
    facts[1] = me
    for copy in scalar_copies:
        copy.wait()
    for at, pair in enumerate(pairs):
        facts[2 + at] = matrix_at(owner, me ^ jnp.where(core == 0, pair[0], pair[1]))
    for s in range(lengths.shape[0]):
        facts[2 + len(pairs) + s] = lengths[s]
    for copy in copies:
        copy.wait()


def load(pairs, owner, lengths, *arrays):
    parts = 4 if all(a.shape[0] % 4 == 0 for a in arrays) else 1
    return pl.pallas_call(
        functools.partial(load_body, pairs),
        out_shape=[pltpu.VMEM(a.shape, a.dtype) for a in arrays]
        + [pltpu.SMEM((2 + len(pairs) + lengths.shape[0],), jnp.int32)],
        in_specs=[HBM] * (2 + len(arrays)),
        out_specs=[VMEM] * len(arrays) + [SMEM],
        scratch_shapes=[
            pltpu.SMEM(owner.shape, jnp.int32),
            pltpu.SMEM(lengths.shape, jnp.int32),
            pltpu.SemaphoreType.DMA((len(arrays), parts)),
            pltpu.SemaphoreType.DMA((2,)),
        ],
        compiler_params=pltpu.CompilerParams(vmem_limit_bytes=4 << 20),
        name="load",
    )(far(owner), far(lengths), *[far(a) for a in arrays])


def whole_body(n, facts, in_v, other_v, out_v, _, *refs):
    grads, tiles = refs[:n], refs[-1]
    half = grads[0].shape[1] // 2
    for at in range(n):

        def store(column, x):
            first = jnp.where(facts[0] == 0, column, (column + half) % (2 * half))
            grads[at][:, pl.ds(pl.multiple_of(first, 128), x.shape[1])] = x

        slot_rows(in_v, other_v, out_v, facts[2 + at], lambda s: facts[2 + n + s], tiles.at[at % 2], store)


def whole_slots(n, facts, in_v, other_in, out_v, passed):
    seqs, _, rows, length = in_v.shape
    width = out_v.shape[2]
    return pl.pallas_call(
        functools.partial(whole_body, n),
        out_shape=[pltpu.VMEM((seqs, 2 * rows * width), jnp.bfloat16)] * n
        + [pltpu.VMEM(passed.shape, passed.dtype)],
        in_specs=[SMEM] + [VMEM] * 4,
        out_specs=[VMEM] * (n + 1),
        input_output_aliases={4: n},
        scratch_shapes=[pltpu.VMEM((2, seqs * (2 * rows + 8), length), jnp.float32)],
        compiler_params=pltpu.CompilerParams(vmem_limit_bytes=12 << 20),
        cost_estimate=pl.CostEstimate(
            flops=4 * n * seqs * rows * width * length,
            bytes_accessed=2 * n * seqs * length * (2 * rows + width),
            transcendentals=0,
        ),
        name="whole_slots",
    )(scalars(facts), here(in_v), here(other_in), here(out_v), here(passed))


def score_body(pairs, facts, ids, *refs):
    n = len(pairs)
    pieces, (own_q, other_q, s_ref, x, t) = refs[:n], refs[n:]
    core, me = facts[0], facts[1]
    seqs, width = pieces[0].shape
    half = width // 2
    total = ids.shape[1]
    own_at = pl.ds(pl.multiple_of(core * half, 128), half)
    other_at = pl.ds(pl.multiple_of((1 - core) * half, 128), half)
    for at, piece in enumerate(pieces):
        x[at * seqs:(at + 1) * seqs, :] = piece[...]
    part = lax.dot_general(x[:, own_at], own_q[...], NT, preferred_element_type=jnp.float32)
    part += lax.dot_general(x[:, other_at], other_q[...], NT, preferred_element_type=jnp.float32)
    t[...] = jnp.zeros_like(t)
    for at, pair in enumerate(pairs):
        rows = (me ^ jnp.where(core == 0, pair[0], pair[1])) * seqs
        t[pl.ds(pl.multiple_of(rows, 16), seqs), :] = part[at * seqs:(at + 1) * seqs].astype(t.dtype)
    wanted = lax.broadcasted_iota(jnp.int32, (total, total), 0)
    pick = jnp.where(wanted == ids[...], 1.0, 0.0).astype(t.dtype)
    s_ref[...] = jnp.dot(pick, t[...], preferred_element_type=jnp.float32).astype(s_ref.dtype)


def partial_scores(pairs, facts, ids, pieces, own_q, other_q):
    seqs, width = pieces[0].shape
    total = ids.shape[1]
    queries = own_q.shape[0]
    args = [*pieces, own_q, other_q]
    rows = len(pairs) * seqs
    return pl.pallas_call(
        functools.partial(score_body, pairs),
        out_shape=jax.ShapeDtypeStruct((total, queries), jnp.bfloat16),
        in_specs=[SMEM] + [VMEM] * (1 + len(args)),
        out_specs=VMEM,
        scratch_shapes=[pltpu.VMEM((rows, width), jnp.bfloat16), pltpu.VMEM((total, queries), jnp.bfloat16)],
        compiler_params=pltpu.CompilerParams(vmem_limit_bytes=16 << 20),
        cost_estimate=pl.CostEstimate(
            flops=2 * rows * queries * width, bytes_accessed=2 * width * (queries + rows), transcendentals=0
        ),
        name="scores",
    )(scalars(facts), ids, *[here(arg) for arg in args])


def fisher_body(total, facts, *refs):
    *pieces, f_hbm, x_ref, left, out, sem = refs
    seqs = pieces[0].shape[0]
    for at, piece in enumerate(pieces):
        x_ref[at * seqs:(at + 1) * seqs, :] = piece[...]
    width = x_ref.shape[1]
    half = width // 2
    depth, block, _ = out.shape
    step = 512 if width % 512 == 0 else width

    def rows_of(i):
        return pl.ds(pl.multiple_of(i * block, block), block)

    def copy(i):
        return pltpu.make_async_copy(out.at[i % depth], f_hbm.at[0, rows_of(i)], sem.at[i % depth])

    def make(i):
        where = pl.ds(pl.multiple_of(facts[0] * half + i * block, 128), block)
        left[rows_of(i), :] = x_ref[:, where].T
        rows = left[rows_of(i), :]
        for at in range(0, width, step):
            tile = jnp.dot(rows, x_ref[:, at:at + step], preferred_element_type=jnp.float32)
            out[i % depth, :, at:at + step] = (tile * (1.0 / total)).astype(out.dtype)
        copy(i).start()

    for i in range(depth):
        make(i)

    @pl.loop(depth, half // block)
    def _(i):
        copy(i - depth).wait()
        make(i)

    for i in range(half // block - depth, half // block):
        copy(i).wait()


def fisher_block(facts, pieces):
    seqs, width = pieces[0].shape
    total, half = len(pieces) * seqs, width // 2
    block, depth = (256, 4) if half % 256 == 0 and half >= 1024 else (half, 1)
    return pl.pallas_call(
        functools.partial(fisher_body, total),
        out_shape=jax.ShapeDtypeStruct((1, half, 2 * half), jnp.bfloat16),
        in_specs=[SMEM] + [VMEM] * len(pieces),
        out_specs=HBM,
        scratch_shapes=[
            pltpu.VMEM((total, width), jnp.bfloat16),
            pltpu.VMEM((half, total), jnp.bfloat16),
            pltpu.VMEM((depth, block, 2 * half), jnp.bfloat16),
            pltpu.SemaphoreType.DMA((depth,)),
        ],
        compiler_params=pltpu.CompilerParams(vmem_limit_bytes=24 << 20),
        cost_estimate=pl.CostEstimate(
            flops=4 * total * half * half, bytes_accessed=4 * half * (half + total), transcendentals=0
        ),
        name="fisher",
    )(scalars(facts), *[here(piece) for piece in pieces])


def local(dp, cores, in_factor, out_factor, seq_lengths, sequence_ids, matrix_owner, queries):
    assert cores == 2 and dp % 4 == 0 and dp & (dp - 1) == 0
    swap = [(0, 1), (1, 0)]
    distant, near = range(dp // 2, dp), range(dp // 2 - 1, -1, -1)
    pairs = []
    for at in range(0, dp // 2, 2):
        pairs += [(distant[at], distant[at + 1]), (near[at], near[at + 1])]
    pairs = tuple(pairs)
    other_in = lax.ppermute(in_factor, "mat", swap)
    in_v, out_v, own_q, facts = load(
        pairs, matrix_owner, seq_lengths, in_factor, out_factor, queries[0]
    )
    *made, own_q = whole_slots(len(pairs), facts, in_v, other_in, out_v, own_q)
    mine = [
        lax.ppermute(
            piece, ("dp", "mat"), [(d * 2 + c, (d ^ pair[c]) * 2 + c) for d in range(dp) for c in range(2)]
        )
        for pair, piece in zip(pairs, made)
    ]
    other_q = lax.ppermute(own_q, "mat", swap)
    theirs = [lax.ppermute(piece, "mat", swap) for piece in mine]
    part = partial_scores(pairs, facts, sequence_ids[None, :], mine, own_q, other_q)
    parts = lax.all_to_all(
        part.reshape(dp * cores, part.shape[0] // (dp * cores), -1),
        ("dp", "mat"),
        split_axis=0,
        concat_axis=0,
        tiled=True,
    )
    fisher = fisher_block(facts, mine + theirs)
    return (fisher, jnp.sum(parts.astype(jnp.float32), axis=0))


def solution(mesh):
    in_specs = (
        P(("groups", "dp"), None, "mat", None),
        P(("groups", "dp"), None, None, None),
        P(("groups", "dp")),
        P("groups"),
        P(),
        P("dp", None, "mat"),
    )
    out_specs = (P(("groups", "dp"), "mat", None), P(("groups", "dp", "mat"), None))
    body = functools.partial(local, mesh.shape["dp"], mesh.shape["mat"])
    return jax.shard_map(body, mesh=mesh, in_specs=in_specs, out_specs=out_specs, check_vma=False)
```

```python
import functools

import jax
import jax.numpy as jnp
from jax import lax
from jax.experimental import pallas as pl
from jax.experimental.pallas import tpu as pltpu
from jax.sharding import PartitionSpec as P

NT = (((1,), (1,)), ((), ()))
VMEM = pl.BlockSpec(memory_space=pltpu.VMEM)
SMEM = pl.BlockSpec(memory_space=pltpu.SMEM)
HBM = pl.BlockSpec(memory_space=pl.ANY)


def here(x):
    return pltpu.with_memory_space_constraint(x, pltpu.VMEM)


def scalars(x):
    return pltpu.with_memory_space_constraint(x, pltpu.SMEM)


def far(x):
    return pltpu.with_memory_space_constraint(x, pltpu.HBM)


def matrix_at(owner, slot):
    matrix = jnp.int32(0)
    for m in range(owner.shape[0]):
        matrix = jnp.where(owner[m] == slot, m, matrix)
    return matrix


def slot_rows(in_v, other_v, out_v, matrix, length_of, tiles, store):
    seqs, _, width, length = out_v.shape
    rows = 2 * in_v.shape[2]
    stride = tiles.shape[0] // (seqs + 1)
    per = length // width
    scale = length ** (-0.5)
    lane = lax.broadcasted_iota(jnp.int32, (1, length), 1)
    for s in range(seqs):
        left = jnp.concatenate([in_v[s, matrix], other_v[s, matrix]], axis=0)
        left = jnp.where(lane < length_of(s), left, 0)
        tile = lax.dot_general(left, out_v[s, matrix], NT, preferred_element_type=jnp.float32)
        tiles[s * stride:s * stride + rows, :] = jnp.concatenate([tile] * per, axis=1)
    for t in range(rows // per):
        tile = tiles[pl.ds(per * t, seqs, stride=stride), :]
        for p in range(1, per):
            other = tiles[pl.ds(per * t + p, seqs, stride=stride), :]
            tile = jnp.where(lane < p * width, tile, other)
        store(t * length, (tile * scale).astype(jnp.bfloat16))


def load_body(pairs, owner_hbm, lengths_hbm, *refs):
    *refs, facts, owner, lengths, sem, small = refs
    n = len(refs) // 2
    parts = sem.shape[1]
    copies = []
    for i in range(n):
        each = refs[i].shape[0] // parts
        for j in range(parts):
            part = pl.ds(j * each, each)
            copies.append(pltpu.make_async_copy(refs[i].at[part], refs[n + i].at[part], sem.at[i, j]))
    scalar_copies = [
        pltpu.make_async_copy(owner_hbm, owner, small.at[0]),
        pltpu.make_async_copy(lengths_hbm, lengths, small.at[1]),
    ]
    for copy in scalar_copies + copies:
        copy.start()
    core, me = lax.axis_index("mat"), lax.axis_index("dp")
    facts[0] = core
    facts[1] = me
    for copy in scalar_copies:
        copy.wait()
    for at, pair in enumerate(pairs):
        facts[2 + at] = matrix_at(owner, me ^ jnp.where(core == 0, pair[0], pair[1]))
    for s in range(lengths.shape[0]):
        facts[2 + len(pairs) + s] = lengths[s]
    for copy in copies:
        copy.wait()


def load(pairs, owner, lengths, *arrays):
    parts = 4 if all(a.shape[0] % 4 == 0 for a in arrays) else 1
    return pl.pallas_call(
        functools.partial(load_body, pairs),
        out_shape=[pltpu.VMEM(a.shape, a.dtype) for a in arrays]
        + [pltpu.SMEM((2 + len(pairs) + lengths.shape[0],), jnp.int32)],
        in_specs=[HBM] * (2 + len(arrays)),
        out_specs=[VMEM] * len(arrays) + [SMEM],
        scratch_shapes=[
            pltpu.SMEM(owner.shape, jnp.int32),
            pltpu.SMEM(lengths.shape, jnp.int32),
            pltpu.SemaphoreType.DMA((len(arrays), parts)),
            pltpu.SemaphoreType.DMA((2,)),
        ],
        compiler_params=pltpu.CompilerParams(vmem_limit_bytes=4 << 20),
        name="load",
    )(far(owner), far(lengths), *[far(a) for a in arrays])


def whole_body(n, facts, in_v, other_v, out_v, _, *refs):
    grads, tiles = refs[:n], refs[-1]
    half = grads[0].shape[1] // 2
    for at in range(n):

        def store(column, x):
            first = jnp.where(facts[0] == 0, column, (column + half) % (2 * half))
            grads[at][:, pl.ds(pl.multiple_of(first, 128), x.shape[1])] = x

        slot_rows(in_v, other_v, out_v, facts[2 + at], lambda s: facts[2 + n + s], tiles.at[at % 2], store)


def whole_slots(n, facts, in_v, other_in, out_v, passed):
    seqs, _, rows, length = in_v.shape
    width = out_v.shape[2]
    return pl.pallas_call(
        functools.partial(whole_body, n),
        out_shape=[pltpu.VMEM((seqs, 2 * rows * width), jnp.bfloat16)] * n
        + [pltpu.VMEM(passed.shape, passed.dtype)],
        in_specs=[SMEM] + [VMEM] * 4,
        out_specs=[VMEM] * (n + 1),
        input_output_aliases={4: n},
        scratch_shapes=[pltpu.VMEM((2, (seqs + 1) * (2 * rows + 8), length), jnp.float32)],
        compiler_params=pltpu.CompilerParams(vmem_limit_bytes=12 << 20),
        cost_estimate=pl.CostEstimate(
            flops=4 * n * seqs * rows * width * length,
            bytes_accessed=2 * n * seqs * length * (2 * rows + width),
            transcendentals=0,
        ),
        name="whole_slots",
    )(scalars(facts), here(in_v), here(other_in), here(out_v), here(passed))


def score_body(pairs, facts, ids, *refs):
    n = len(pairs)
    pieces, (own_q, other_q, s_ref, x, t) = refs[:n], refs[n:]
    core, me = facts[0], facts[1]
    seqs, width = pieces[0].shape
    half = width // 2
    total = ids.shape[1]
    own_at = pl.ds(pl.multiple_of(core * half, 128), half)
    other_at = pl.ds(pl.multiple_of((1 - core) * half, 128), half)
    for at, piece in enumerate(pieces):
        x[at * seqs:(at + 1) * seqs, :] = piece[...]
    part = lax.dot_general(x[:, own_at], own_q[...], NT, preferred_element_type=jnp.float32)
    part += lax.dot_general(x[:, other_at], other_q[...], NT, preferred_element_type=jnp.float32)
    t[...] = jnp.zeros_like(t)
    for at, pair in enumerate(pairs):
        rows = (me ^ jnp.where(core == 0, pair[0], pair[1])) * seqs
        t[pl.ds(pl.multiple_of(rows, 16), seqs), :] = part[at * seqs:(at + 1) * seqs].astype(t.dtype)
    wanted = lax.broadcasted_iota(jnp.int32, (total, total), 0)
    pick = jnp.where(wanted == ids[...], 1.0, 0.0).astype(t.dtype)
    s_ref[...] = jnp.dot(pick, t[...], preferred_element_type=jnp.float32).astype(s_ref.dtype)


def partial_scores(pairs, facts, ids, pieces, own_q, other_q):
    seqs, width = pieces[0].shape
    total = ids.shape[1]
    queries = own_q.shape[0]
    args = [*pieces, own_q, other_q]
    rows = len(pairs) * seqs
    return pl.pallas_call(
        functools.partial(score_body, pairs),
        out_shape=jax.ShapeDtypeStruct((total, queries), jnp.bfloat16),
        in_specs=[SMEM] + [VMEM] * (1 + len(args)),
        out_specs=VMEM,
        scratch_shapes=[pltpu.VMEM((rows, width), jnp.bfloat16), pltpu.VMEM((total, queries), jnp.bfloat16)],
        compiler_params=pltpu.CompilerParams(vmem_limit_bytes=16 << 20),
        cost_estimate=pl.CostEstimate(
            flops=2 * rows * queries * width, bytes_accessed=2 * width * (queries + rows), transcendentals=0
        ),
        name="scores",
    )(scalars(facts), ids, *[here(arg) for arg in args])


def fisher_body(total, facts, *refs):
    *pieces, f_hbm, x_ref, left, out, sem = refs
    seqs = pieces[0].shape[0]
    for at, piece in enumerate(pieces):
        x_ref[at * seqs:(at + 1) * seqs, :] = piece[...]
    width = x_ref.shape[1]
    half = width // 2
    depth, block, _ = out.shape
    step = 512 if width % 512 == 0 else width

    def rows_of(i):
        return pl.ds(pl.multiple_of(i * block, block), block)

    def copy(i):
        return pltpu.make_async_copy(out.at[i % depth], f_hbm.at[0, rows_of(i)], sem.at[i % depth])

    def make(i):
        where = pl.ds(pl.multiple_of(facts[0] * half + i * block, 128), block)
        left[rows_of(i), :] = x_ref[:, where].T
        rows = left[rows_of(i), :]
        for at in range(0, width, step):
            tile = jnp.dot(rows, x_ref[:, at:at + step], preferred_element_type=jnp.float32)
            out[i % depth, :, at:at + step] = (tile * (1.0 / total)).astype(out.dtype)
        copy(i).start()

    for i in range(depth):
        make(i)

    @pl.loop(depth, half // block)
    def _(i):
        copy(i - depth).wait()
        make(i)

    for i in range(half // block - depth, half // block):
        copy(i).wait()


def fisher_block(facts, pieces):
    seqs, width = pieces[0].shape
    total, half = len(pieces) * seqs, width // 2
    block, depth = (256, 4) if half % 256 == 0 and half >= 1024 else (half, 1)
    return pl.pallas_call(
        functools.partial(fisher_body, total),
        out_shape=jax.ShapeDtypeStruct((1, half, 2 * half), jnp.bfloat16),
        in_specs=[SMEM] + [VMEM] * len(pieces),
        out_specs=HBM,
        scratch_shapes=[
            pltpu.VMEM((total, width), jnp.bfloat16),
            pltpu.VMEM((half, total), jnp.bfloat16),
            pltpu.VMEM((depth, block, 2 * half), jnp.bfloat16),
            pltpu.SemaphoreType.DMA((depth,)),
        ],
        compiler_params=pltpu.CompilerParams(vmem_limit_bytes=24 << 20),
        cost_estimate=pl.CostEstimate(
            flops=4 * total * half * half, bytes_accessed=4 * half * (half + total), transcendentals=0
        ),
        name="fisher",
    )(scalars(facts), *[here(piece) for piece in pieces])


def local(dp, cores, in_factor, out_factor, seq_lengths, sequence_ids, matrix_owner, queries):
    assert cores == 2 and dp % 4 == 0 and dp & (dp - 1) == 0
    swap = [(0, 1), (1, 0)]
    distant, near = range(dp // 2, dp), range(dp // 2 - 1, -1, -1)
    pairs = []
    for at in range(0, dp // 2, 2):
        pairs += [(distant[at], distant[at + 1]), (near[at], near[at + 1])]
    pairs = tuple(pairs)
    other_in = lax.ppermute(in_factor, "mat", swap)
    in_v, out_v, own_q, facts = load(
        pairs, matrix_owner, seq_lengths, in_factor, out_factor, queries[0]
    )
    *made, own_q = whole_slots(len(pairs), facts, in_v, other_in, out_v, own_q)
    mine = [
        lax.ppermute(
            piece, ("dp", "mat"), [(d * 2 + c, (d ^ pair[c]) * 2 + c) for d in range(dp) for c in range(2)]
        )
        for pair, piece in zip(pairs, made)
    ]
    other_q = lax.ppermute(own_q, "mat", swap)
    theirs = [lax.ppermute(piece, "mat", swap) for piece in mine]
    part = partial_scores(pairs, facts, sequence_ids[None, :], mine, own_q, other_q)
    parts = lax.all_to_all(
        part.reshape(dp * cores, part.shape[0] // (dp * cores), -1),
        ("dp", "mat"),
        split_axis=0,
        concat_axis=0,
        tiled=True,
    )
    fisher = fisher_block(facts, mine + theirs)
    return (fisher, jnp.sum(parts.astype(jnp.float32), axis=0))


def solution(mesh):
    in_specs = (
        P(("groups", "dp"), None, "mat", None),
        P(("groups", "dp"), None, None, None),
        P(("groups", "dp")),
        P("groups"),
        P(),
        P("dp", None, "mat"),
    )
    out_specs = (P(("groups", "dp"), "mat", None), P(("groups", "dp", "mat"), None))
    body = functools.partial(local, mesh.shape["dp"], mesh.shape["mat"])
    return jax.shard_map(body, mesh=mesh, in_specs=in_specs, out_specs=out_specs, check_vma=False)
```

```python
import functools

import jax
import jax.numpy as jnp
from jax import lax
from jax.experimental import pallas as pl
from jax.experimental.pallas import tpu as pltpu
from jax.sharding import PartitionSpec as P

NT = (((1,), (1,)), ((), ()))
VMEM = pl.BlockSpec(memory_space=pltpu.VMEM)
SMEM = pl.BlockSpec(memory_space=pltpu.SMEM)
HBM = pl.BlockSpec(memory_space=pl.ANY)


def here(x):
    return pltpu.with_memory_space_constraint(x, pltpu.VMEM)


def scalars(x):
    return pltpu.with_memory_space_constraint(x, pltpu.SMEM)


def far(x):
    return pltpu.with_memory_space_constraint(x, pltpu.HBM)


def matrix_at(owner, slot):
    matrix = jnp.int32(0)
    for m in range(owner.shape[0]):
        matrix = jnp.where(owner[m] == slot, m, matrix)
    return matrix


def slot_rows(in_v, other_v, out_v, matrix, length_of, tiles, store):
    seqs, _, width, length = out_v.shape
    rows = 2 * in_v.shape[2]
    stride = tiles.shape[0] // (seqs + 1)
    per = length // width
    scale = length ** (-0.5)
    lane = lax.broadcasted_iota(jnp.int32, (1, length), 1)
    for s in range(seqs):
        left = jnp.concatenate([in_v[s, matrix], other_v[s, matrix]], axis=0)
        left = jnp.where(lane < length_of(s), left, 0)
        tile = lax.dot_general(left, out_v[s, matrix], NT, preferred_element_type=jnp.float32)
        tiles[s * stride:s * stride + rows, :] = jnp.concatenate([tile] * per, axis=1)
    for t in range(rows // per):
        tile = tiles[pl.ds(per * t, seqs, stride=stride), :]
        for p in range(1, per):
            other = tiles[pl.ds(per * t + p, seqs, stride=stride), :]
            tile = jnp.where(lane < p * width, tile, other)
        store(t * length, (tile * scale).astype(jnp.bfloat16))


def load_body(pairs, owner_hbm, lengths_hbm, *refs):
    *refs, facts, owner, lengths, sem, small = refs
    n = len(refs) // 2
    parts = sem.shape[1]
    copies = []
    for i in range(n):
        each = refs[i].shape[0] // parts
        for j in range(parts):
            part = pl.ds(j * each, each)
            copies.append(pltpu.make_async_copy(refs[i].at[part], refs[n + i].at[part], sem.at[i, j]))
    scalar_copies = [
        pltpu.make_async_copy(owner_hbm, owner, small.at[0]),
        pltpu.make_async_copy(lengths_hbm, lengths, small.at[1]),
    ]
    for copy in scalar_copies + copies:
        copy.start()
    core, me = lax.axis_index("mat"), lax.axis_index("dp")
    facts[0] = core
    facts[1] = me
    for copy in scalar_copies:
        copy.wait()
    for at, pair in enumerate(pairs):
        facts[2 + at] = matrix_at(owner, me ^ jnp.where(core == 0, pair[0], pair[1]))
    for s in range(lengths.shape[0]):
        facts[2 + len(pairs) + s] = lengths[s]
    for copy in copies:
        copy.wait()


def load(pairs, owner, lengths, *arrays):
    parts = 4 if all(a.shape[0] % 4 == 0 for a in arrays) else 1
    return pl.pallas_call(
        functools.partial(load_body, pairs),
        out_shape=[pltpu.VMEM(a.shape, a.dtype) for a in arrays]
        + [pltpu.SMEM((2 + len(pairs) + lengths.shape[0],), jnp.int32)],
        in_specs=[HBM] * (2 + len(arrays)),
        out_specs=[VMEM] * len(arrays) + [SMEM],
        scratch_shapes=[
            pltpu.SMEM(owner.shape, jnp.int32),
            pltpu.SMEM(lengths.shape, jnp.int32),
            pltpu.SemaphoreType.DMA((len(arrays), parts)),
            pltpu.SemaphoreType.DMA((2,)),
        ],
        compiler_params=pltpu.CompilerParams(vmem_limit_bytes=4 << 20),
        name="load",
    )(far(owner), far(lengths), *[far(a) for a in arrays])


def whole_body(n, facts, in_v, other_v, out_v, _, *refs):
    grads, tiles = refs[:n], refs[-1]
    half = grads[0].shape[1] // 2
    for at in range(n):

        def store(column, x):
            first = jnp.where(facts[0] == 0, column, (column + half) % (2 * half))
            grads[at][:, pl.ds(pl.multiple_of(first, 128), x.shape[1])] = x

        slot_rows(in_v, other_v, out_v, facts[2 + at], lambda s: facts[2 + n + s], tiles.at[at % 2], store)


def whole_slots(n, facts, in_v, other_in, out_v, passed):
    seqs, _, rows, length = in_v.shape
    width = out_v.shape[2]
    return pl.pallas_call(
        functools.partial(whole_body, n),
        out_shape=[pltpu.VMEM((seqs, 2 * rows * width), jnp.bfloat16)] * n
        + [pltpu.VMEM(passed.shape, passed.dtype)],
        in_specs=[SMEM] + [VMEM] * 4,
        out_specs=[VMEM] * (n + 1),
        input_output_aliases={4: n},
        scratch_shapes=[pltpu.VMEM((2, (seqs + 1) * (2 * rows + 8), length), jnp.float32)],
        compiler_params=pltpu.CompilerParams(vmem_limit_bytes=12 << 20),
        cost_estimate=pl.CostEstimate(
            flops=4 * n * seqs * rows * width * length,
            bytes_accessed=2 * n * seqs * length * (2 * rows + width),
            transcendentals=0,
        ),
        name="whole_slots",
    )(scalars(facts), here(in_v), here(other_in), here(out_v), here(passed))


def score_body(pairs, facts, ids, *refs):
    n = len(pairs)
    pieces, (own_q, other_q, s_ref, x, t) = refs[:n], refs[n:]
    core, me = facts[0], facts[1]
    seqs, width = pieces[0].shape
    half = width // 2
    total = ids.shape[1]
    own_at = pl.ds(pl.multiple_of(core * half, 128), half)
    other_at = pl.ds(pl.multiple_of((1 - core) * half, 128), half)
    for at, piece in enumerate(pieces):
        x[at * seqs:(at + 1) * seqs, :] = piece[...]
    part = lax.dot_general(x[:, own_at], own_q[...], NT, preferred_element_type=jnp.float32)
    part += lax.dot_general(x[:, other_at], other_q[...], NT, preferred_element_type=jnp.float32)
    t[...] = jnp.zeros_like(t)
    for at, pair in enumerate(pairs):
        rows = (me ^ jnp.where(core == 0, pair[0], pair[1])) * seqs
        t[pl.ds(pl.multiple_of(rows, 16), seqs), :] = part[at * seqs:(at + 1) * seqs].astype(t.dtype)
    at = lax.broadcasted_iota(jnp.int32, (total, total), 0)
    each = seqs // 2
    wanted = at % (total // 2) // each * seqs + at // (total // 2) * each + at % each
    pick = jnp.where(wanted == ids[...], 1.0, 0.0).astype(t.dtype)
    s_ref[...] = jnp.dot(pick, t[...], preferred_element_type=jnp.float32).astype(s_ref.dtype)


def partial_scores(pairs, facts, ids, pieces, own_q, other_q):
    seqs, width = pieces[0].shape
    total = ids.shape[1]
    queries = own_q.shape[0]
    args = [*pieces, own_q, other_q]
    rows = len(pairs) * seqs
    return pl.pallas_call(
        functools.partial(score_body, pairs),
        out_shape=jax.ShapeDtypeStruct((total, queries), jnp.bfloat16),
        in_specs=[SMEM] + [VMEM] * (1 + len(args)),
        out_specs=VMEM,
        scratch_shapes=[pltpu.VMEM((rows, width), jnp.bfloat16), pltpu.VMEM((total, queries), jnp.bfloat16)],
        compiler_params=pltpu.CompilerParams(vmem_limit_bytes=16 << 20),
        cost_estimate=pl.CostEstimate(
            flops=2 * rows * queries * width, bytes_accessed=2 * width * (queries + rows), transcendentals=0
        ),
        name="scores",
    )(scalars(facts), ids, *[here(arg) for arg in args])


def fisher_body(total, facts, *refs):
    *pieces, f_hbm, x_ref, left, out, sem = refs
    seqs = pieces[0].shape[0]
    for at, piece in enumerate(pieces):
        x_ref[at * seqs:(at + 1) * seqs, :] = piece[...]
    width = x_ref.shape[1]
    half = width // 2
    depth, block, _ = out.shape
    step = 512 if width % 512 == 0 else width

    def rows_of(i):
        return pl.ds(pl.multiple_of(i * block, block), block)

    def copy(i):
        return pltpu.make_async_copy(out.at[i % depth], f_hbm.at[0, rows_of(i)], sem.at[i % depth])

    def make(i):
        where = pl.ds(pl.multiple_of(facts[0] * half + i * block, 128), block)
        left[rows_of(i), :] = x_ref[:, where].T
        rows = left[rows_of(i), :]
        for at in range(0, width, step):
            tile = jnp.dot(rows, x_ref[:, at:at + step], preferred_element_type=jnp.float32)
            out[i % depth, :, at:at + step] = (tile * (1.0 / total)).astype(out.dtype)
        copy(i).start()

    for i in range(depth):
        make(i)

    @pl.loop(depth, half // block)
    def _(i):
        copy(i - depth).wait()
        make(i)

    for i in range(half // block - depth, half // block):
        copy(i).wait()


def fisher_block(facts, pieces):
    seqs, width = pieces[0].shape
    total, half = len(pieces) * seqs, width // 2
    block, depth = (256, 4) if half % 256 == 0 and half >= 1024 else (half, 1)
    return pl.pallas_call(
        functools.partial(fisher_body, total),
        out_shape=jax.ShapeDtypeStruct((1, half, 2 * half), jnp.bfloat16),
        in_specs=[SMEM] + [VMEM] * len(pieces),
        out_specs=HBM,
        scratch_shapes=[
            pltpu.VMEM((total, width), jnp.bfloat16),
            pltpu.VMEM((half, total), jnp.bfloat16),
            pltpu.VMEM((depth, block, 2 * half), jnp.bfloat16),
            pltpu.SemaphoreType.DMA((depth,)),
        ],
        compiler_params=pltpu.CompilerParams(vmem_limit_bytes=24 << 20),
        cost_estimate=pl.CostEstimate(
            flops=4 * total * half * half, bytes_accessed=4 * half * (half + total), transcendentals=0
        ),
        name="fisher",
    )(scalars(facts), *[here(piece) for piece in pieces])


def local(dp, cores, in_factor, out_factor, seq_lengths, sequence_ids, matrix_owner, queries):
    assert cores == 2 and dp % 4 == 0 and dp & (dp - 1) == 0
    swap = [(0, 1), (1, 0)]
    distant, near = range(dp // 2, dp), range(dp // 2 - 1, -1, -1)
    pairs = []
    for at in range(0, dp // 2, 2):
        pairs += [(distant[at], distant[at + 1]), (near[at], near[at + 1])]
    pairs = tuple(pairs)
    other_in = lax.ppermute(in_factor, "mat", swap)
    in_v, out_v, own_q, facts = load(
        pairs, matrix_owner, seq_lengths, in_factor, out_factor, queries[0]
    )
    *made, own_q = whole_slots(len(pairs), facts, in_v, other_in, out_v, own_q)
    mine = [
        lax.ppermute(
            piece, ("dp", "mat"), [(d * 2 + c, (d ^ pair[c]) * 2 + c) for d in range(dp) for c in range(2)]
        )
        for pair, piece in zip(pairs, made)
    ]
    other_q = lax.ppermute(own_q, "mat", swap)
    theirs = [lax.ppermute(piece, "mat", swap) for piece in mine]
    part = partial_scores(pairs, facts, sequence_ids[None, :], mine, own_q, other_q)
    parts = lax.all_to_all(
        part.reshape(dp * cores, part.shape[0] // (dp * cores), -1),
        ("mat", "dp"),
        split_axis=0,
        concat_axis=0,
        tiled=True,
    )
    fisher = fisher_block(facts, mine + theirs)
    return (fisher, jnp.sum(parts.astype(jnp.float32), axis=0))


def solution(mesh):
    in_specs = (
        P(("groups", "dp"), None, "mat", None),
        P(("groups", "dp"), None, None, None),
        P(("groups", "dp")),
        P("groups"),
        P(),
        P("dp", None, "mat"),
    )
    out_specs = (P(("groups", "dp"), "mat", None), P(("groups", "dp", "mat"), None))
    body = functools.partial(local, mesh.shape["dp"], mesh.shape["mat"])
    return jax.shard_map(body, mesh=mesh, in_specs=in_specs, out_specs=out_specs, check_vma=False)
```
